32 devices in a mesh: basin: 2 (over y), row: 4 (over z), col: 4 (over x, core).
Axes of the slice: x: 2, y: 2, z: 4, core: 2. Of those that a mesh axis runs over, the one named last changes fastest.
Arguments:
- wet_mask: int32 [512, 4096], P(('basin', 'row'), 'col'), parts along dimension 0, may hold values 0 or 1
- land_class: int32 [512, 4096], P(('basin', 'row'), 'col'), parts along dimension 0, may hold values from 0 to 15
- flood_label: int32 [512, 4096], P(('basin', 'row'), 'col'), parts along dimension 0, may hold values 0 or 1
- conductance: float32 [16], replicated, may hold values from 0.5 to 3
- storage: float32 [512, 4096], P(('basin', 'row'), 'col'), parts along dimension 0, may hold values from 0.1 to 1
- prior_depth: float32 [512, 4096], P(('basin', 'row'), 'col'), parts along dimension 0, may hold values from -6 to 6
- rainfall: float32 [512, 4096], P(('basin', 'row'), 'col'), parts along dimension 0, may hold values from -6 to 6
Outputs:
- depth_iterate: float32 [512, 4096], P(('basin', 'row'), 'col'), parts along dimension 0
- adjoint_iterate: float32 [512, 4096], P(('basin', 'row'), 'col'), parts along dimension 0
The draws below stay inside these ranges and needn't reach their ends.
There are 2 independent parts, one for each index of `basin`. The reference program is written for one: setup_inputs(seed, part) draws one part's arguments, and reference() takes and returns one part's arrays. A program takes and returns all parts, laid end to end along the dimension named above; an argument that names none is the same for every part. Nothing has to cross between parts.
All inputs are finite; a program needn't handle non-finite values. No bound on the sum of `wet_mask` or of `flood_label` on one device may be relied on, other than what follows from the above.
Results may differ from the reference program's by a relative error of at most 0.00015.
Values sent between devices are 32-bit elements; how exact they have to be, the bound alone decides.
A program may use at most 64 MiB of HBM per device.

```python
import math
import jax
import jax.numpy as jnp

NCLASS = 16
ITERS = 3
NR = 256
NC = 4096


def touch_ends(values, stream_key, smallest, top_value):
    dims = values.shape
    place = [jax.random.randint(jax.random.fold_in(stream_key, axis), (), 0, dims[axis]) for axis in range(len(dims))]
    values = values.at[tuple(place)].set(smallest)
    longest = dims.index(max(dims))
    place[longest] = (place[longest] + 1) % dims[longest]
    return values.at[tuple(place)].set(top_value)


def shard_levels(stream_key, dims, shards, smallest, top_value):
    loudness = 1.0
    for axis_at, shards_of in shards:
        draws = jax.random.uniform(jax.random.fold_in(jax.random.fold_in(stream_key, 6), axis_at), (shards_of,), jnp.float32, smallest / len(shards), top_value / len(shards))
        loudness = loudness * jnp.repeat(jnp.exp(draws), dims[axis_at] // shards_of).reshape((-1,) + (1,) * (len(dims) - 1 - axis_at))
    return loudness


def noise(rng, dims, width, most, pieces=(), kind=jnp.bfloat16):
    factor_of = shard_levels(rng, dims, pieces, -0.22, 0.18) if pieces else 1.0
    values = jax.random.normal(rng, dims, jnp.float32) * width * factor_of
    return jnp.minimum(jnp.maximum(values, -most), most).astype(kind)


def setup_inputs(seed: int = 0, part: int = 0) -> dict:
    seeds = jax.random.split(jax.random.key(seed), 8)
    own_keys = jax.random.split(jax.random.fold_in(seeds[7], part), 8)
    return {
        "wet_mask": touch_ends((jax.random.randint(own_keys[0], (NR, NC), 0, 4) < 3).astype(jnp.int32), jax.random.fold_in(own_keys[0], 1), 0, 1),
        "land_class": touch_ends(jax.random.randint(own_keys[1], (NR, NC), 0, NCLASS), jax.random.fold_in(own_keys[1], 1), 0, NCLASS - 1).astype(jnp.int32),
        "flood_label": touch_ends((jax.random.randint(own_keys[2], (NR, NC), 0, 2) < 1).astype(jnp.int32), jax.random.fold_in(own_keys[2], 1), 0, 1),
        "conductance": jnp.clip(jnp.exp(jax.random.uniform(seeds[3], (NCLASS,), jnp.float32, math.log(0.5), math.log(3.0))), 0.5, 3.0),
        "storage": jnp.clip(jnp.exp(math.log(1.0) - 2.3025851 * jax.random.uniform(own_keys[4], (NR, NC), jnp.float32) ** shard_levels(own_keys[4], (NR, NC), ((0, 4), (1, 4)), -0.2, 0.2)), 0.1, 1.0),
        "prior_depth": noise(own_keys[5], (NR, NC), 1.0, 6.0, ((0, 4), (1, 4)), jnp.float32),
        "rainfall": noise(own_keys[6], (NR, NC), 1.0, 6.0, ((0, 4), (1, 4)), jnp.float32),
    }


def build_operator(cell, storage):
    padded = jnp.pad(cell, 1)
    k_up = cell * padded[:-2, 1:-1]
    k_down = cell * padded[2:, 1:-1]
    k_left = cell * padded[1:-1, :-2]
    k_right = cell * padded[1:-1, 2:]
    diagonal = storage + k_up + k_down + k_left + k_right
    return diagonal, k_up, k_down, k_left, k_right


def operate(field, coeffs):
    diagonal, k_up, k_down, k_left, k_right = coeffs
    padded = jnp.pad(field, ((0, 0), (1, 1), (1, 1)))
    return (diagonal * field - k_up * padded[:, :-2, 1:-1] - k_down * padded[:, 2:, 1:-1]
            - k_left * padded[:, 1:-1, :-2] - k_right * padded[:, 1:-1, 2:])


def reference(wet_mask, land_class, flood_label, conductance, storage, prior_depth, rainfall):
    wet = wet_mask.astype(jnp.float32)
    cell = conductance[land_class] * wet
    coeffs = build_operator(cell, storage)
    forward_side = storage * prior_depth + wet * rainfall
    adjoint_side = wet * (jax.nn.sigmoid(prior_depth) - flood_label.astype(jnp.float32))
    right = jnp.stack([forward_side, adjoint_side])
    solution = jnp.zeros_like(right)
    residual = right
    direction = right
    norm_now = jnp.sum(residual * residual, axis=(1, 2))
    for step in range(ITERS):
        image = operate(direction, coeffs)
        alpha = norm_now / jnp.sum(direction * image, axis=(1, 2))
        solution = solution + alpha[:, None, None] * direction
        residual = residual - alpha[:, None, None] * image
        norm_next = jnp.sum(residual * residual, axis=(1, 2))
        direction = residual + (norm_next / norm_now)[:, None, None] * direction
        norm_now = norm_next
    return solution[0], solution[1]
```

```python
import functools

import jax
import jax.numpy as jnp
from jax import lax
from jax.experimental import pallas as pl
from jax.experimental.pallas import tpu as pltpu
from jax.sharding import PartitionSpec as P

MESH = pl.DeviceIdType.MESH
LANES = 128
SUB = 8
PIECE = 4
STEPS = (
    (-1, 0), (1, 0), (0, -1), (0, 1), (-1, -1), (-1, 1), (1, -1), (1, 1),
)
OPPOSITE = (1, 0, 3, 2, 7, 6, 5, 4)


def lookup(index, table):
    values = [table[i] for i in range(table.shape[0])]
    bit = 1
    while len(values) > 1:
        odd = (index & bit) != 0
        values = [jnp.where(odd, values[i + 1], values[i]) for i in range(0, len(values), 2)]
        bit *= 2
    return values[0]


def iota(shape, dim):
    return lax.broadcasted_iota(jnp.int32, shape, dim)


def fold(values):
    rows, lanes = values.shape
    return values.reshape(rows // SUB, SUB, lanes).sum(axis=0)


def coefficients(m, c):
    n = [c * m[k] + m[k + 1] for k in range(5)]
    a0 = m[0] / n[0]
    r0, r1 = 1.0 - a0 * c, -a0
    rr1 = r0 * r0 * m[0] + 2.0 * r0 * r1 * m[1] + r1 * r1 * m[2]
    p0, p1 = r0 + rr1 / m[0], r1
    curve = p0 * p0 * n[0] + 2.0 * p0 * p1 * n[1] + p1 * p1 * n[2]
    a1 = rr1 / curve
    u0, u1 = a0 + a1 * p0, a1 * p1
    r0, r1, r2 = r0 - a1 * c * p0, r1 - a1 * (p0 + c * p1), -a1 * p1
    rr2 = (r0 * r0 * m[0] + 2.0 * r0 * r1 * m[1] + (r1 * r1 + 2.0 * r0 * r2) * m[2]
           + 2.0 * r1 * r2 * m[3] + r2 * r2 * m[4])
    beta = rr2 / rr1
    p0, p1, p2 = r0 + beta * p0, r1 + beta * p1, r2
    curve = (p0 * p0 * n[0] + 2.0 * p0 * p1 * n[1] + (p1 * p1 + 2.0 * p0 * p2) * n[2]
             + 2.0 * p1 * p2 * n[3] + p2 * p2 * n[4])
    a2 = rr2 / curve
    return u0 + a2 * p0, u1 + a2 * p1, a2 * p2


def kernel(
    nrow, ncol, stages,
    wet_h, land_h, label_h, cond, stor_h, prior_h, rain_h, out0_h, out1_h,
    wet_v, land_v, label_v, stor_v, prior_v, rain_v, out_v,
    v0, v1, v2, cell_s, diag_s,
    pack_rows, pack_cols, got_rows, got_cols, part, got_part,
    in_sem, out_sem, send_sem, recv_sem, psend_sem, precv_sem,
):
    rows, cols = stor_v.shape
    nb, npan = rows // SUB, cols // LANES
    row, col = lax.axis_index("row"), lax.axis_index("col")

    loads = [
        pltpu.make_async_copy(src, dst, in_sem.at[i])
        for i, (src, dst) in enumerate((
            (land_h, land_v), (wet_h, wet_v), (stor_h, stor_v),
            (prior_h, prior_v), (rain_h, rain_v), (label_h, label_v)))
    ]
    for load in loads:
        load.start()

    got_rows[...] = jnp.zeros_like(got_rows)
    got_cols[...] = jnp.zeros_like(got_cols)

    there = []
    for dr, dc in STEPS:
        ok = True
        for at, d, n in ((row, dr, nrow), (col, dc, ncol)):
            if d:
                here = (at > 0) if d < 0 else (at < n - 1)
                ok = here if ok is True else jnp.logical_and(ok, here)
        there.append(ok)

    def place(k):
        dr, dc = STEPS[k]
        return {"row": row + dr, "col": col + dc}

    def peer(stage, k):
        if stage == "both":
            at = lax.rem(row * ncol + col + k, nrow * ncol)
            return {"row": at // ncol, "col": lax.rem(at, ncol)}
        if stage == "col":
            return {"row": row, "col": lax.rem(col + k, ncol)}
        return {"row": lax.rem(row + k, nrow), "col": col}

    counts = {"both": nrow * ncol, "row": nrow, "col": ncol}
    barrier = pltpu.get_barrier_semaphore()
    expect = 0
    for stage in stages:
        for k in range(1, counts[stage]):
            pl.semaphore_signal(barrier, inc=1, device_id=peer(stage, k), device_id_type=MESH)
        expect += counts[stage] - 1
    if "both" not in stages:
        for k in range(4, 8):
            @pl.when(there[k])
            def _():
                pl.semaphore_signal(barrier, inc=1, device_id=place(k), device_id_type=MESH)
            expect = expect + there[k].astype(jnp.int32)

    shift = cond[0]
    for i in range(1, cond.shape[0]):
        shift = shift + cond[i]
    shift = shift * (2.0 / cond.shape[0])
    shift = shift * shift

    for load in loads:
        load.wait()
    for j in range(npan):
        at = pl.ds(j * LANES, LANES)
        wet = wet_v[:, at].astype(jnp.float32)
        prior = prior_v[:, at]
        stor = stor_v[:, at]
        core = pl.ds(0, rows)
        cell_s[j, core, :] = lookup(land_v[:, at], cond) * wet
        v0[0, j, core, :] = stor * prior + wet * rain_v[:, at]
        v0[1, j, core, :] = wet * (1.0 / (1.0 + jnp.exp(-prior)) - label_v[:, at].astype(jnp.float32))
        diag_s[j, core, :] = stor

    fields = (v0.at[0], v0.at[1], cell_s, diag_s)
    sub = iota((SUB, LANES), 0)
    lane = iota((SUB, LANES), 1)
    upper = sub < PIECE
    halves = lane < LANES // 2

    for pair in range(2):
        fa, fb = fields[2 * pair], fields[2 * pair + 1]
        for j in range(npan):
            top = pl.ds(0, SUB)
            bottom = pl.ds(rows - SUB, SUB)
            pack_rows[0, pair, j] = jnp.where(upper, fa[j, top, :], pltpu.roll(fb[j, top, :], PIECE, 0))
            pack_rows[1, pair, j] = jnp.where(upper, pltpu.roll(fa[j, bottom, :], PIECE, 0), fb[j, bottom, :])

    left = jnp.zeros((SUB, LANES), jnp.float32)
    right = jnp.zeros((SUB, LANES), jnp.float32)
    slot = lane // PIECE
    for f, field in enumerate(fields):
        for r in range(nb):
            k = f * nb + r
            block = pl.ds(r * SUB, SUB)
            left = jnp.where(slot == k, pltpu.roll(field[0, block, :], PIECE * k, 1), left)
            right = jnp.where(
                slot == k, pltpu.roll(field[npan - 1, block, :], (PIECE * k + PIECE) % LANES, 1), right)
    pack_cols[0] = left
    pack_cols[1] = right

    pl.semaphore_wait(barrier, expect)

    def halo(k, arriving):
        dr, dc = STEPS[k]
        to = k if arriving else OPPOSITE[k]
        if dc == 0:
            src, dst = pack_rows.at[k], got_rows.at[to]
        else:
            src, dst = pack_cols.at[(dc + 1) // 2], got_cols.at[to - 2]
        return pltpu.make_async_remote_copy(
            src_ref=src, dst_ref=dst, send_sem=send_sem.at[k], recv_sem=recv_sem.at[to],
            device_id=place(k), device_id_type=MESH)

    for k in range(8):
        @pl.when(there[k])
        def _():
            halo(k, False).start()
    for k in range(8):
        @pl.when(there[k])
        def _():
            halo(k, True).wait_recv()

    tail = pl.ds(rows, SUB)
    for f, field in enumerate(fields):
        pair, second = f // 2, f % 2
        for j in range(npan):
            after, before = got_rows[1, pair, j], got_rows[0, pair, j]
            if second:
                after = pltpu.roll(after, PIECE, 0)
            else:
                before = pltpu.roll(before, PIECE, 0)
            field[j, tail, :] = jnp.where(upper, after, before)

        def side(after, before, r):
            k = f * nb + r
            after = pltpu.roll(after, (LANES - PIECE * k) % LANES, 1)
            before = pltpu.roll(before, LANES - PIECE - PIECE * k, 1)
            return jnp.where(halves, after, before)

        for r in range(nb):
            field[npan, pl.ds(r * SUB, SUB), :] = side(got_cols[1], got_cols[0], r)
        field[npan, tail, :] = jnp.where(
            upper, side(got_cols[5], got_cols[4], 0), side(got_cols[3], got_cols[2], nb - 1))

    tall = rows + SUB
    first = iota((tall, LANES), 1) == 0
    last = iota((tall, LANES), 1) == LANES - 1

    def around(panels):
        total = npan + 1
        fwd = [pltpu.roll(w, 1, 1) for w in panels]
        bwd = [pltpu.roll(w, LANES - 1, 1) for w in panels]
        for j in range(total):
            w = panels[j]
            yield (pltpu.roll(w, 1, 0) + pltpu.roll(w, tall - 1, 0)
                   + jnp.where(first, fwd[(j - 1) % total], fwd[j])
                   + jnp.where(last, bwd[(j + 1) % total], bwd[j]))

    for j, s in enumerate(around([cell_s[j] for j in range(npan + 1)])):
        diag_s[j] = diag_s[j] + cell_s[j] * s - shift

    def dots(a, b, total):
        term = fold(a[:rows] * b[:rows])
        return term if total is None else total + term

    moments = []
    for s in range(2):
        m = [None] * 6
        for step, (src, dst) in enumerate(((v0, v1), (v1, v2), (v2, None))):
            weighted = [cell_s[j] * src[s, j] for j in range(npan + 1)]
            for j, near in enumerate(around(weighted)):
                if dst is None and j == npan:
                    continue
                field = src[s, j]
                image = diag_s[j] * field - cell_s[j] * near
                if dst is not None:
                    dst[s, j] = image
                if j < npan:
                    if step == 0:
                        m[0] = dots(field, field, m[0])
                    m[2 * step + 1] = dots(field, image, m[2 * step + 1])
                    if step < 2:
                        m[2 * step + 2] = dots(image, image, m[2 * step + 2])
        moments.append(m)

    gap = jnp.zeros((2, LANES), jnp.float32)
    spread = [jnp.sum(x, axis=0, keepdims=True) for x in moments[0]] + [gap]
    spread += [jnp.sum(x, axis=0, keepdims=True) for x in moments[1]] + [gap]
    spread = jnp.concatenate(spread, axis=0)
    on = iota((2 * SUB, LANES), 0) == iota((2 * SUB, LANES), 1)
    sums = jnp.sum(spread, axis=1, keepdims=True)
    sums = jnp.sum(jnp.where(on, sums, 0.0), axis=0, keepdims=True)

    base = 0
    for number, stage in enumerate(stages):
        part[number] = sums
        copies = []
        for k in range(1, counts[stage]):
            copies.append(pltpu.make_async_remote_copy(
                src_ref=part.at[number], dst_ref=got_part.at[base + k],
                send_sem=psend_sem.at[base + k], recv_sem=precv_sem.at[base + k],
                device_id=peer(stage, k), device_id_type=MESH))
            copies[-1].start()
        for copy in copies:
            copy.wait_recv()
        for k in range(1, counts[stage]):
            sums = sums + got_part[base + k]
        for copy in copies:
            copy.wait_send()
        base += counts[stage]

    sums = jnp.sum(jnp.where(on, sums, 0.0), axis=1, keepdims=True)
    sums = jnp.broadcast_to(sums, (2 * SUB, LANES))
    stores = []
    for s, out_h in enumerate((out0_h, out1_h)):
        m = [sums[s * SUB + i:s * SUB + i + 1] for i in range(6)]
        e0, e1, e2 = coefficients(m, shift)
        for j in range(npan):
            core = pl.ds(0, rows)
            out_v[s, :, pl.ds(j * LANES, LANES)] = (
                e0 * v0[s, j, core, :] + e1 * v1[s, j, core, :] + e2 * v2[s, j, core, :])
        stores.append(pltpu.make_async_copy(out_v.at[s], out_h, out_sem.at[s]))
        stores[-1].start()
    for k in range(8):
        @pl.when(there[k])
        def _():
            halo(k, False).wait_send()
    for store in stores:
        store.wait()


def body(nrow, ncol, wet_mask, land_class, flood_label, conductance, storage, prior_depth, rainfall):
    rows, cols = storage.shape
    nb, npan = rows // SUB, cols // LANES
    stages = ("both",) if nrow * ncol <= 32 else ("col", "row")
    slots = nrow * ncol if len(stages) == 1 else nrow + ncol
    f32, i32 = jnp.float32, jnp.int32
    tile = (rows, cols)
    padded = (npan + 1, rows + SUB, LANES)
    hbm = pl.BlockSpec(memory_space=pl.ANY)
    return pl.pallas_call(
        functools.partial(kernel, nrow, ncol, stages),
        out_shape=(jax.ShapeDtypeStruct(tile, f32), jax.ShapeDtypeStruct(tile, f32)),
        in_specs=[hbm, hbm, hbm, pl.BlockSpec(memory_space=pltpu.SMEM), hbm, hbm, hbm],
        out_specs=(hbm, hbm),
        scratch_shapes=[
            pltpu.VMEM(tile, i32), pltpu.VMEM(tile, i32), pltpu.VMEM(tile, i32),
            pltpu.VMEM(tile, f32), pltpu.VMEM(tile, f32), pltpu.VMEM(tile, f32),
            pltpu.VMEM((2,) + tile, f32),
            pltpu.VMEM((2,) + padded, f32), pltpu.VMEM((2,) + padded, f32), pltpu.VMEM((2,) + padded, f32),
            pltpu.VMEM(padded, f32), pltpu.VMEM(padded, f32),
            pltpu.VMEM((2, 2, npan, SUB, LANES), f32), pltpu.VMEM((2, SUB, LANES), f32),
            pltpu.VMEM((2, 2, npan, SUB, LANES), f32), pltpu.VMEM((6, SUB, LANES), f32),
            pltpu.VMEM((2, 1, LANES), f32), pltpu.VMEM((slots, 1, LANES), f32),
            pltpu.SemaphoreType.DMA((6,)), pltpu.SemaphoreType.DMA((2,)),
            pltpu.SemaphoreType.DMA((8,)), pltpu.SemaphoreType.DMA((8,)),
            pltpu.SemaphoreType.DMA((slots,)), pltpu.SemaphoreType.DMA((slots,)),
        ],
        compiler_params=pltpu.CompilerParams(
            collective_id=0, has_side_effects=True, vmem_limit_bytes=32 * 1024 * 1024),
        name="moments",
    )(wet_mask, land_class, flood_label, conductance, storage, prior_depth, rainfall)


def solution(mesh):
    spread = P(("basin", "row"), "col")
    return jax.shard_map(
        functools.partial(body, mesh.shape["row"], mesh.shape["col"]),
        mesh=mesh,
        in_specs=(spread, spread, spread, P(), spread, spread, spread),
        out_specs=(spread, spread),
        check_vma=False,
    )
```

```python
import functools

import jax
import jax.numpy as jnp
from jax import lax
from jax.experimental import pallas as pl
from jax.experimental.pallas import tpu as pltpu
from jax.sharding import PartitionSpec as P

MESH = pl.DeviceIdType.MESH
LANES = 128
SUB = 8
PIECE = 4
LIMIT = 63500 * 1024
STEPS = (
    (-1, 0), (1, 0), (0, -1), (0, 1), (-1, -1), (-1, 1), (1, -1), (1, 1),
)
OPPOSITE = (1, 0, 3, 2, 7, 6, 5, 4)


def lookup(index, table):
    values = [table[i] for i in range(table.shape[0])]
    bit = 1
    while len(values) > 1:
        odd = (index & bit) != 0
        values = [jnp.where(odd, values[i + 1], values[i]) for i in range(0, len(values), 2)]
        bit *= 2
    return values[0]


def iota(shape, dim):
    return lax.broadcasted_iota(jnp.int32, shape, dim)


def fold(values):
    rows, lanes = values.shape
    return values.reshape(rows // SUB, SUB, lanes).sum(axis=0)


def coefficients(m, c):
    n = [c * m[k] + m[k + 1] for k in range(5)]
    a0 = m[0] / n[0]
    r0, r1 = 1.0 - a0 * c, -a0
    rr1 = r0 * r0 * m[0] + 2.0 * r0 * r1 * m[1] + r1 * r1 * m[2]
    p0, p1 = r0 + rr1 / m[0], r1
    curve = p0 * p0 * n[0] + 2.0 * p0 * p1 * n[1] + p1 * p1 * n[2]
    a1 = rr1 / curve
    u0, u1 = a0 + a1 * p0, a1 * p1
    r0, r1, r2 = r0 - a1 * c * p0, r1 - a1 * (p0 + c * p1), -a1 * p1
    rr2 = (r0 * r0 * m[0] + 2.0 * r0 * r1 * m[1] + (r1 * r1 + 2.0 * r0 * r2) * m[2]
           + 2.0 * r1 * r2 * m[3] + r2 * r2 * m[4])
    beta = rr2 / rr1
    p0, p1, p2 = r0 + beta * p0, r1 + beta * p1, r2
    curve = (p0 * p0 * n[0] + 2.0 * p0 * p1 * n[1] + (p1 * p1 + 2.0 * p0 * p2) * n[2]
             + 2.0 * p1 * p2 * n[3] + p2 * p2 * n[4])
    a2 = rr2 / curve
    return u0 + a2 * p0, u1 + a2 * p1, a2 * p2


def kernel(
    nrow, ncol, stages,
    wet_h, land_h, label_h, cond_h, stor_h, prior_h, rain_h, out0_h, out1_h,
    wet_v, land_v, label_v, stor_v, prior_v, rain_v, cond, out_v,
    v0, v1, v2, cell_s, diag_s,
    pack_rows, pack_cols, got_rows, got_cols, part, got_part,
    in_sem, out_sem, send_sem, recv_sem, psend_sem, precv_sem,
):
    rows, cols = stor_v.shape
    nb, npan = rows // SUB, cols // LANES
    row, col = lax.axis_index("row"), lax.axis_index("col")

    loads = [
        pltpu.make_async_copy(src, dst, in_sem.at[i])
        for i, (src, dst) in enumerate((
            (land_h, land_v), (wet_h, wet_v), (stor_h, stor_v),
            (prior_h, prior_v), (rain_h, rain_v), (label_h, label_v), (cond_h, cond)))
    ]
    for load in loads:
        load.start()

    got_rows[...] = jnp.zeros_like(got_rows)
    got_cols[...] = jnp.zeros_like(got_cols)

    there = []
    for dr, dc in STEPS:
        ok = True
        for at, d, n in ((row, dr, nrow), (col, dc, ncol)):
            if d:
                here = (at > 0) if d < 0 else (at < n - 1)
                ok = here if ok is True else jnp.logical_and(ok, here)
        there.append(ok)

    def place(k):
        dr, dc = STEPS[k]
        return {"row": row + dr, "col": col + dc}

    def peer(stage, k):
        if stage == "both":
            at = lax.rem(row * ncol + col + k, nrow * ncol)
            return {"row": at // ncol, "col": lax.rem(at, ncol)}
        if stage == "col":
            return {"row": row, "col": lax.rem(col + k, ncol)}
        return {"row": lax.rem(row + k, nrow), "col": col}

    counts = {"both": nrow * ncol, "row": nrow, "col": ncol}
    barrier = pltpu.get_barrier_semaphore()
    expect = 0
    for stage in stages:
        for k in range(1, counts[stage]):
            pl.semaphore_signal(barrier, inc=1, device_id=peer(stage, k), device_id_type=MESH)
        expect += counts[stage] - 1
    if "both" not in stages:
        for k in range(4, 8):
            @pl.when(there[k])
            def _():
                pl.semaphore_signal(barrier, inc=1, device_id=place(k), device_id_type=MESH)
            expect = expect + there[k].astype(jnp.int32)

    for load in loads:
        load.wait()
    shift = cond[0]
    for i in range(1, cond.shape[0]):
        shift = shift + cond[i]
    shift = shift * (2.0 / cond.shape[0])
    shift = shift * shift

    for j in range(npan):
        at = pl.ds(j * LANES, LANES)
        wet = wet_v[:, at].astype(jnp.float32)
        prior = prior_v[:, at]
        stor = stor_v[:, at]
        core = pl.ds(0, rows)
        cell_s[j, core, :] = lookup(land_v[:, at], cond) * wet
        v0[0, j, core, :] = stor * prior + wet * rain_v[:, at]
        v0[1, j, core, :] = wet * (1.0 / (1.0 + jnp.exp(-prior)) - label_v[:, at].astype(jnp.float32))
        diag_s[j, core, :] = stor

    fields = (v0.at[0], v0.at[1], cell_s, diag_s)
    sub = iota((SUB, LANES), 0)
    lane = iota((SUB, LANES), 1)
    upper = sub < PIECE
    halves = lane < LANES // 2

    for pair in range(2):
        fa, fb = fields[2 * pair], fields[2 * pair + 1]
        for j in range(npan):
            top = pl.ds(0, SUB)
            bottom = pl.ds(rows - SUB, SUB)
            pack_rows[0, pair, j] = jnp.where(upper, fa[j, top, :], pltpu.roll(fb[j, top, :], PIECE, 0))
            pack_rows[1, pair, j] = jnp.where(upper, pltpu.roll(fa[j, bottom, :], PIECE, 0), fb[j, bottom, :])

    left = jnp.zeros((SUB, LANES), jnp.float32)
    right = jnp.zeros((SUB, LANES), jnp.float32)
    slot = lane // PIECE
    for f, field in enumerate(fields):
        for r in range(nb):
            k = f * nb + r
            block = pl.ds(r * SUB, SUB)
            left = jnp.where(slot == k, pltpu.roll(field[0, block, :], PIECE * k, 1), left)
            right = jnp.where(
                slot == k, pltpu.roll(field[npan - 1, block, :], (PIECE * k + PIECE) % LANES, 1), right)
    pack_cols[0] = left
    pack_cols[1] = right

    pl.semaphore_wait(barrier, expect)

    def halo(k, arriving):
        dr, dc = STEPS[k]
        to = k if arriving else OPPOSITE[k]
        if dc == 0:
            src, dst = pack_rows.at[k], got_rows.at[to]
        else:
            src, dst = pack_cols.at[(dc + 1) // 2], got_cols.at[to - 2]
        return pltpu.make_async_remote_copy(
            src_ref=src, dst_ref=dst, send_sem=send_sem.at[k], recv_sem=recv_sem.at[to],
            device_id=place(k), device_id_type=MESH)

    for k in range(8):
        @pl.when(there[k])
        def _():
            halo(k, False).start()
    for k in range(8):
        @pl.when(there[k])
        def _():
            halo(k, True).wait_recv()

    tail = pl.ds(rows, SUB)
    for f, field in enumerate(fields):
        pair, second = f // 2, f % 2
        for j in range(npan):
            after, before = got_rows[1, pair, j], got_rows[0, pair, j]
            if second:
                after = pltpu.roll(after, PIECE, 0)
            else:
                before = pltpu.roll(before, PIECE, 0)
            field[j, tail, :] = jnp.where(upper, after, before)

        def side(after, before, r):
            k = f * nb + r
            after = pltpu.roll(after, (LANES - PIECE * k) % LANES, 1)
            before = pltpu.roll(before, LANES - PIECE - PIECE * k, 1)
            return jnp.where(halves, after, before)

        for r in range(nb):
            field[npan, pl.ds(r * SUB, SUB), :] = side(got_cols[1], got_cols[0], r)
        field[npan, tail, :] = jnp.where(
            upper, side(got_cols[5], got_cols[4], 0), side(got_cols[3], got_cols[2], nb - 1))

    tall = rows + SUB
    first = iota((tall, LANES), 1) == 0
    last = iota((tall, LANES), 1) == LANES - 1

    def around(panels):
        total = npan + 1
        fwd = [pltpu.roll(w, 1, 1) for w in panels]
        bwd = [pltpu.roll(w, LANES - 1, 1) for w in panels]
        for j in range(total):
            w = panels[j]
            yield (pltpu.roll(w, 1, 0) + pltpu.roll(w, tall - 1, 0)
                   + jnp.where(first, fwd[(j - 1) % total], fwd[j])
                   + jnp.where(last, bwd[(j + 1) % total], bwd[j]))

    for j, s in enumerate(around([cell_s[j] for j in range(npan + 1)])):
        diag_s[j] = diag_s[j] + cell_s[j] * s - shift

    def dots(a, b, total):
        term = fold(a[:rows] * b[:rows])
        return term if total is None else total + term

    moments = []
    for s in range(2):
        m = [None] * 6
        for step, (src, dst) in enumerate(((v0, v1), (v1, v2), (v2, None))):
            weighted = [cell_s[j] * src[s, j] for j in range(npan + 1)]
            for j, near in enumerate(around(weighted)):
                if dst is None and j == npan:
                    continue
                field = src[s, j]
                image = diag_s[j] * field - cell_s[j] * near
                if dst is not None:
                    dst[s, j] = image
                if j < npan:
                    if step == 0:
                        m[0] = dots(field, field, m[0])
                    m[2 * step + 1] = dots(field, image, m[2 * step + 1])
                    if step < 2:
                        m[2 * step + 2] = dots(image, image, m[2 * step + 2])
        moments.append(m)

    gap = jnp.zeros((2, LANES), jnp.float32)
    spread = [jnp.sum(x, axis=0, keepdims=True) for x in moments[0]] + [gap]
    spread += [jnp.sum(x, axis=0, keepdims=True) for x in moments[1]] + [gap]
    spread = jnp.concatenate(spread, axis=0)
    on = iota((2 * SUB, LANES), 0) == iota((2 * SUB, LANES), 1)
    sums = jnp.sum(spread, axis=1, keepdims=True)
    sums = jnp.sum(jnp.where(on, sums, 0.0), axis=0, keepdims=True)

    base = 0
    for number, stage in enumerate(stages):
        part[number] = sums
        copies = []
        for k in range(1, counts[stage]):
            copies.append(pltpu.make_async_remote_copy(
                src_ref=part.at[number], dst_ref=got_part.at[base + k],
                send_sem=psend_sem.at[base + k], recv_sem=precv_sem.at[base + k],
                device_id=peer(stage, k), device_id_type=MESH))
            copies[-1].start()
        for copy in copies:
            copy.wait_recv()
        for k in range(1, counts[stage]):
            sums = sums + got_part[base + k]
        for copy in copies:
            copy.wait_send()
        base += counts[stage]

    sums = jnp.sum(jnp.where(on, sums, 0.0), axis=1, keepdims=True)
    sums = jnp.broadcast_to(sums, (2 * SUB, LANES))
    stores = []
    for s, out_h in enumerate((out0_h, out1_h)):
        m = [sums[s * SUB + i:s * SUB + i + 1] for i in range(6)]
        e0, e1, e2 = coefficients(m, shift)
        for half in range(2):
            low = half * (rows // 2)
            core = pl.ds(low, rows // 2)
            for j in range(npan):
                out_v[s, core, pl.ds(j * LANES, LANES)] = (
                    e0 * v0[s, j, core, :] + e1 * v1[s, j, core, :] + e2 * v2[s, j, core, :])
            stores.append(pltpu.make_async_copy(out_v.at[s, core], out_h.at[core], out_sem.at[2 * s + half]))
            stores[-1].start()
    for k in range(8):
        @pl.when(there[k])
        def _():
            halo(k, False).wait_send()
    for store in stores:
        store.wait()


def hand_over(a_h, b_h, out0_h, out1_h, held, sem, out_sem):
    loads, stores = [], []
    for s, (src, dst) in enumerate(((a_h, out0_h), (b_h, out1_h))):
        for h in range(2):
            at = pl.ds(h * (src.shape[0] // 2), src.shape[0] // 2)
            loads.append(pltpu.make_async_copy(src.at[at], held.at[s, at], sem.at[s, h]))
            stores.append(pltpu.make_async_copy(held.at[s, at], dst.at[at], out_sem.at[s, h]))
            loads[-1].start()
    for load, store in zip(loads, stores):
        load.wait()
        store.start()
    for store in stores:
        store.wait()


def body(nrow, ncol, wet_mask, land_class, flood_label, conductance, storage, prior_depth, rainfall):
    rows, cols = storage.shape
    nb, npan = rows // SUB, cols // LANES
    stages = ("both",) if nrow * ncol <= 32 else ("col", "row")
    slots = nrow * ncol if len(stages) == 1 else nrow + ncol
    f32, i32 = jnp.float32, jnp.int32
    tile = (rows, cols)
    table = conductance.shape[0]
    padded = (npan + 1, rows + SUB, LANES)
    hbm = pl.BlockSpec(memory_space=pltpu.HBM)
    near = pl.BlockSpec(memory_space=pl.ANY)
    outs = pl.pallas_call(
        functools.partial(kernel, nrow, ncol, stages),
        out_shape=(jax.ShapeDtypeStruct(tile, f32), jax.ShapeDtypeStruct(tile, f32)),
        in_specs=[hbm] * 7,
        out_specs=(near, near),
        scratch_shapes=[
            pltpu.VMEM(tile, i32), pltpu.VMEM(tile, i32), pltpu.VMEM(tile, i32),
            pltpu.VMEM(tile, f32), pltpu.VMEM(tile, f32), pltpu.VMEM(tile, f32),
            pltpu.SMEM((table,), f32), pltpu.VMEM((2,) + tile, f32),
            pltpu.VMEM((2,) + padded, f32), pltpu.VMEM((2,) + padded, f32), pltpu.VMEM((2,) + padded, f32),
            pltpu.VMEM(padded, f32), pltpu.VMEM(padded, f32),
            pltpu.VMEM((2, 2, npan, SUB, LANES), f32), pltpu.VMEM((2, SUB, LANES), f32),
            pltpu.VMEM((2, 2, npan, SUB, LANES), f32), pltpu.VMEM((6, SUB, LANES), f32),
            pltpu.VMEM((2, 1, LANES), f32), pltpu.VMEM((slots, 1, LANES), f32),
            pltpu.SemaphoreType.DMA((7,)), pltpu.SemaphoreType.DMA((4,)),
            pltpu.SemaphoreType.DMA((8,)), pltpu.SemaphoreType.DMA((8,)),
            pltpu.SemaphoreType.DMA((slots,)), pltpu.SemaphoreType.DMA((slots,)),
        ],
        compiler_params=pltpu.CompilerParams(
            collective_id=0, has_side_effects=True, vmem_limit_bytes=LIMIT),
        name="moments",
    )(wet_mask, land_class, flood_label, conductance, storage, prior_depth, rainfall)
    return pl.pallas_call(
        hand_over,
        out_shape=(jax.ShapeDtypeStruct(tile, f32), jax.ShapeDtypeStruct(tile, f32)),
        in_specs=[near, near],
        out_specs=(near, near),
        scratch_shapes=[pltpu.VMEM((2,) + tile, f32), pltpu.SemaphoreType.DMA((2, 2)), pltpu.SemaphoreType.DMA((2, 2))],
        compiler_params=pltpu.CompilerParams(vmem_limit_bytes=LIMIT),
        name="hand_over",
    )(*outs)


def solution(mesh):
    spread = P(("basin", "row"), "col")
    return jax.shard_map(
        functools.partial(body, mesh.shape["row"], mesh.shape["col"]),
        mesh=mesh,
        in_specs=(spread, spread, spread, P(), spread, spread, spread),
        out_specs=(spread, spread),
        check_vma=False,
    )
```

```python
import functools

import jax
import jax.numpy as jnp
from jax import lax
from jax.experimental import pallas as pl
from jax.experimental.pallas import tpu as pltpu
from jax.sharding import PartitionSpec as P

MESH = pl.DeviceIdType.MESH
LANES = 128
SUB = 8
PIECE = 4
LIMIT = 63500 * 1024
STEPS = (
    (-1, 0), (1, 0), (0, -1), (0, 1), (-1, -1), (-1, 1), (1, -1), (1, 1),
)
OPPOSITE = (1, 0, 3, 2, 7, 6, 5, 4)


def lookup(index, table):
    values = [table[i] for i in range(table.shape[0])]
    bit = 1
    while len(values) > 1:
        odd = (index & bit) != 0
        values = [jnp.where(odd, values[i + 1], values[i]) for i in range(0, len(values), 2)]
        bit *= 2
    return values[0]


def iota(shape, dim):
    return lax.broadcasted_iota(jnp.int32, shape, dim)


def fold(values):
    rows, lanes = values.shape
    return values.reshape(rows // SUB, SUB, lanes).sum(axis=0)


def coefficients(m, c):
    n = [c * m[k] + m[k + 1] for k in range(5)]
    a0 = m[0] / n[0]
    r0, r1 = 1.0 - a0 * c, -a0
    rr1 = r0 * r0 * m[0] + 2.0 * r0 * r1 * m[1] + r1 * r1 * m[2]
    p0, p1 = r0 + rr1 / m[0], r1
    curve = p0 * p0 * n[0] + 2.0 * p0 * p1 * n[1] + p1 * p1 * n[2]
    a1 = rr1 / curve
    u0, u1 = a0 + a1 * p0, a1 * p1
    r0, r1, r2 = r0 - a1 * c * p0, r1 - a1 * (p0 + c * p1), -a1 * p1
    rr2 = (r0 * r0 * m[0] + 2.0 * r0 * r1 * m[1] + (r1 * r1 + 2.0 * r0 * r2) * m[2]
           + 2.0 * r1 * r2 * m[3] + r2 * r2 * m[4])
    beta = rr2 / rr1
    p0, p1, p2 = r0 + beta * p0, r1 + beta * p1, r2
    curve = (p0 * p0 * n[0] + 2.0 * p0 * p1 * n[1] + (p1 * p1 + 2.0 * p0 * p2) * n[2]
             + 2.0 * p1 * p2 * n[3] + p2 * p2 * n[4])
    a2 = rr2 / curve
    return u0 + a2 * p0, u1 + a2 * p1, a2 * p2


def kernel(
    nrow, ncol, stages,
    wet_h, land_h, label_h, cond_h, stor_h, prior_h, rain_h, out0_h, out1_h,
    wet_v, land_v, label_v, stor_v, prior_v, rain_v, cond, out_v,
    v0, v1, v2, cell_s, diag_s, diag_in,
    pack_rows, pack_cols, got_rows, got_cols, part, got_part,
    in_sem, out_sem, send_sem, recv_sem, psend_sem, precv_sem,
):
    rows, cols = stor_v.shape
    nb, npan = rows // SUB, cols // LANES
    row, col = lax.axis_index("row"), lax.axis_index("col")

    loads = [
        pltpu.make_async_copy(src, dst, in_sem.at[i])
        for i, (src, dst) in enumerate((
            (land_h, land_v), (wet_h, wet_v), (stor_h, stor_v),
            (prior_h, prior_v), (rain_h, rain_v), (label_h, label_v), (cond_h, cond)))
    ]
    for load in loads:
        load.start()

    got_rows[...] = jnp.zeros_like(got_rows)
    got_cols[...] = jnp.zeros_like(got_cols)

    there = []
    for dr, dc in STEPS:
        ok = True
        for at, d, n in ((row, dr, nrow), (col, dc, ncol)):
            if d:
                here = (at > 0) if d < 0 else (at < n - 1)
                ok = here if ok is True else jnp.logical_and(ok, here)
        there.append(ok)

    def place(k):
        dr, dc = STEPS[k]
        return {"row": row + dr, "col": col + dc}

    def peer(stage, k):
        if stage == "both":
            at = lax.rem(row * ncol + col + k, nrow * ncol)
            return {"row": at // ncol, "col": lax.rem(at, ncol)}
        if stage == "col":
            return {"row": row, "col": lax.rem(col + k, ncol)}
        return {"row": lax.rem(row + k, nrow), "col": col}

    counts = {"both": nrow * ncol, "row": nrow, "col": ncol}
    barrier = pltpu.get_barrier_semaphore()
    expect = 0
    for stage in stages:
        for k in range(1, counts[stage]):
            pl.semaphore_signal(barrier, inc=1, device_id=peer(stage, k), device_id_type=MESH)
        expect += counts[stage] - 1
    if "both" not in stages:
        for k in range(4, 8):
            @pl.when(there[k])
            def _():
                pl.semaphore_signal(barrier, inc=1, device_id=place(k), device_id_type=MESH)
            expect = expect + there[k].astype(jnp.int32)

    for load in loads:
        load.wait()
    shift = cond[0]
    for i in range(1, cond.shape[0]):
        shift = shift + cond[i]
    shift = shift * (2.0 / cond.shape[0])
    shift = shift * shift

    for j in range(npan):
        at = pl.ds(j * LANES, LANES)
        wet = wet_v[:, at].astype(jnp.float32)
        prior = prior_v[:, at]
        stor = stor_v[:, at]
        core = pl.ds(0, rows)
        cell_s[j, core, :] = lookup(land_v[:, at], cond) * wet
        v0[0, j, core, :] = stor * prior + wet * rain_v[:, at]
        v0[1, j, core, :] = wet * (1.0 / (1.0 + jnp.exp(-prior)) - label_v[:, at].astype(jnp.float32))
        diag_s[j, core, :] = stor

    fields = (v0.at[0], v0.at[1], cell_s, diag_s)
    sub = iota((SUB, LANES), 0)
    lane = iota((SUB, LANES), 1)
    upper = sub < PIECE
    halves = lane < LANES // 2

    for pair in range(2):
        fa, fb = fields[2 * pair], fields[2 * pair + 1]
        for j in range(npan):
            top = pl.ds(0, SUB)
            bottom = pl.ds(rows - SUB, SUB)
            pack_rows[0, pair, j] = jnp.where(upper, fa[j, top, :], pltpu.roll(fb[j, top, :], PIECE, 0))
            pack_rows[1, pair, j] = jnp.where(upper, pltpu.roll(fa[j, bottom, :], PIECE, 0), fb[j, bottom, :])

    left = jnp.zeros((SUB, LANES), jnp.float32)
    right = jnp.zeros((SUB, LANES), jnp.float32)
    slot = lane // PIECE
    for f, field in enumerate(fields):
        for r in range(nb):
            k = f * nb + r
            block = pl.ds(r * SUB, SUB)
            left = jnp.where(slot == k, pltpu.roll(field[0, block, :], PIECE * k, 1), left)
            right = jnp.where(
                slot == k, pltpu.roll(field[npan - 1, block, :], (PIECE * k + PIECE) % LANES, 1), right)
    pack_cols[0] = left
    pack_cols[1] = right

    pl.semaphore_wait(barrier, expect)

    def halo(k, arriving):
        dr, dc = STEPS[k]
        to = k if arriving else OPPOSITE[k]
        if dc == 0:
            src, dst = pack_rows.at[k], got_rows.at[to]
        else:
            src, dst = pack_cols.at[(dc + 1) // 2], got_cols.at[to - 2]
        return pltpu.make_async_remote_copy(
            src_ref=src, dst_ref=dst, send_sem=send_sem.at[k], recv_sem=recv_sem.at[to],
            device_id=place(k), device_id_type=MESH)

    for k in range(8):
        @pl.when(there[k])
        def _():
            halo(k, False).start()
    def around(panels):
        tall, total = panels[0].shape[0], len(panels)
        first = iota((tall, LANES), 1) == 0
        last = iota((tall, LANES), 1) == LANES - 1
        fwd = [pltpu.roll(w, 1, 1) for w in panels]
        bwd = [pltpu.roll(w, LANES - 1, 1) for w in panels]
        return [
            pltpu.roll(w, 1, 0) + pltpu.roll(w, tall - 1, 0)
            + jnp.where(first, fwd[(j - 1) % total], fwd[j])
            + jnp.where(last, bwd[(j + 1) % total], bwd[j])
            for j, w in enumerate(panels)
        ]

    def dots(a, b, total):
        term = fold(a * b)
        return term if total is None else total + term

    def gather(m, step, field, image):
        if step == 0:
            m[0] = dots(field, field, m[0])
        m[2 * step + 1] = dots(field, image, m[2 * step + 1])
        if step < 2:
            m[2 * step + 2] = dots(image, image, m[2 * step + 2])

    whole = pl.ds(0, rows)
    middle = pl.ds(SUB, rows - 2 * SUB)
    inside = slice(SUB, rows - SUB)
    nears = around([cell_s[j, whole, :] for j in range(npan)])
    for j in range(npan):
        diag_in[j] = diag_s[j, whole, :] + cell_s[j, whole, :] * nears[j] - shift
    moments = [[None] * 6, [None] * 6]
    for s in range(2):
        for step, (src, dst) in enumerate(((v0, v1), (v1, v2), (v2, None))):
            nears = around([cell_s[j, whole, :] * src[s, j, whole, :] for j in range(npan)])
            for j in range(npan):
                deep = 0 < j < npan - 1
                if dst is None and not deep:
                    continue
                field = src[s, j, whole, :]
                image = diag_in[j] * field - cell_s[j, whole, :] * nears[j]
                if dst is not None:
                    dst[s, j, whole, :] = image
                if deep:
                    gather(moments[s], step, field[inside], image[inside])

    for k in range(8):
        @pl.when(there[k])
        def _():
            halo(k, True).wait_recv()

    tail = pl.ds(rows, SUB)
    for f, field in enumerate(fields):
        pair, second = f // 2, f % 2
        for j in range(npan):
            after, before = got_rows[1, pair, j], got_rows[0, pair, j]
            if second:
                after = pltpu.roll(after, PIECE, 0)
            else:
                before = pltpu.roll(before, PIECE, 0)
            field[j, tail, :] = jnp.where(upper, after, before)

        def side(after, before, r):
            k = f * nb + r
            after = pltpu.roll(after, (LANES - PIECE * k) % LANES, 1)
            before = pltpu.roll(before, LANES - PIECE - PIECE * k, 1)
            return jnp.where(halves, after, before)

        for r in range(nb):
            field[npan, pl.ds(r * SUB, SUB), :] = side(got_cols[1], got_cols[0], r)
        field[npan, tail, :] = jnp.where(
            upper, side(got_cols[5], got_cols[4], 0), side(got_cols[3], got_cols[2], nb - 1))

    ring = [npan - 2, npan - 1, npan, 0, 1]

    def wide(field, j):
        return jnp.concatenate(
            [field[j, pl.ds(rows - 2 * SUB, 3 * SUB), :], field[j, pl.ds(0, 2 * SUB), :]], axis=0)

    def narrow(field, j):
        return jnp.concatenate(
            [field[j, pl.ds(rows - SUB, 2 * SUB), :], field[j, pl.ds(0, SUB), :]], axis=0)

    def put(field, j, value):
        field[j, pl.ds(rows - SUB, 2 * SUB), :] = value[:2 * SUB]
        field[j, pl.ds(0, SUB), :] = value[2 * SUB:]

    def ends(value):
        return jnp.concatenate([value[:SUB], value[2 * SUB:]], axis=0)

    nears = around([wide(cell_s, j) for j in range(npan + 1)])
    for j in range(npan + 1):
        value = narrow(diag_s, j) + narrow(cell_s, j) * nears[j][SUB:4 * SUB] - shift
        put(diag_s, j, value)
    nears = around([cell_s[j, whole, :] for j in ring])
    for j, near in zip(ring[1:4], nears[1:4]):
        diag_s[j, middle, :] = diag_s[j, middle, :] + cell_s[j, middle, :] * near[SUB:rows - SUB] - shift
    for s in range(2):
        m = moments[s]
        for step, (src, dst) in enumerate(((v0, v1), (v1, v2), (v2, None))):
            nears = around([wide(cell_s, j) * wide(src.at[s], j) for j in range(npan + 1)])
            for j in range(npan + 1):
                if dst is None and j == npan:
                    continue
                field = narrow(src.at[s], j)
                image = narrow(diag_s, j) * field - narrow(cell_s, j) * nears[j][SUB:4 * SUB]
                if dst is not None:
                    put(dst.at[s], j, image)
                if j < npan:
                    gather(m, step, ends(field), ends(image))
            nears = around([cell_s[j, whole, :] * src[s, j, whole, :] for j in ring])
            for j, near in zip(ring[1:4], nears[1:4]):
                if dst is None and j == npan:
                    continue
                field = src[s, j, middle, :]
                image = diag_s[j, middle, :] * field - cell_s[j, middle, :] * near[SUB:rows - SUB]
                if dst is not None:
                    dst[s, j, middle, :] = image
                if j < npan:
                    gather(m, step, field, image)

    gap = jnp.zeros((2, LANES), jnp.float32)
    spread = [jnp.sum(x, axis=0, keepdims=True) for x in moments[0]] + [gap]
    spread += [jnp.sum(x, axis=0, keepdims=True) for x in moments[1]] + [gap]
    spread = jnp.concatenate(spread, axis=0)
    on = iota((2 * SUB, LANES), 0) == iota((2 * SUB, LANES), 1)
    sums = jnp.sum(spread, axis=1, keepdims=True)
    sums = jnp.sum(jnp.where(on, sums, 0.0), axis=0, keepdims=True)

    base = 0
    for number, stage in enumerate(stages):
        part[number] = sums
        copies = []
        for k in range(1, counts[stage]):
            copies.append(pltpu.make_async_remote_copy(
                src_ref=part.at[number], dst_ref=got_part.at[base + k],
                send_sem=psend_sem.at[base + k], recv_sem=precv_sem.at[base + k],
                device_id=peer(stage, k), device_id_type=MESH))
            copies[-1].start()
        for copy in copies:
            copy.wait_recv()
        for k in range(1, counts[stage]):
            sums = sums + got_part[base + k]
        for copy in copies:
            copy.wait_send()
        base += counts[stage]

    sums = jnp.sum(jnp.where(on, sums, 0.0), axis=1, keepdims=True)
    sums = jnp.broadcast_to(sums, (2 * SUB, LANES))
    stores = []
    for s, out_h in enumerate((out0_h, out1_h)):
        m = [sums[s * SUB + i:s * SUB + i + 1] for i in range(6)]
        e0, e1, e2 = coefficients(m, shift)
        for half in range(2):
            low = half * (rows // 2)
            core = pl.ds(low, rows // 2)
            for j in range(npan):
                out_v[s, core, pl.ds(j * LANES, LANES)] = (
                    e0 * v0[s, j, core, :] + e1 * v1[s, j, core, :] + e2 * v2[s, j, core, :])
            stores.append(pltpu.make_async_copy(out_v.at[s, core], out_h.at[core], out_sem.at[2 * s + half]))
            stores[-1].start()
    for k in range(8):
        @pl.when(there[k])
        def _():
            halo(k, False).wait_send()
    for store in stores:
        store.wait()


def hand_over(a_h, b_h, out0_h, out1_h, held, sem, out_sem):
    loads, stores = [], []
    for s, (src, dst) in enumerate(((a_h, out0_h), (b_h, out1_h))):
        for h in range(2):
            at = pl.ds(h * (src.shape[0] // 2), src.shape[0] // 2)
            loads.append(pltpu.make_async_copy(src.at[at], held.at[s, at], sem.at[s, h]))
            stores.append(pltpu.make_async_copy(held.at[s, at], dst.at[at], out_sem.at[s, h]))
            loads[-1].start()
    for load, store in zip(loads, stores):
        load.wait()
        store.start()
    for store in stores:
        store.wait()


def body(nrow, ncol, wet_mask, land_class, flood_label, conductance, storage, prior_depth, rainfall):
    rows, cols = storage.shape
    nb, npan = rows // SUB, cols // LANES
    stages = ("both",) if nrow * ncol <= 32 else ("col", "row")
    slots = nrow * ncol if len(stages) == 1 else nrow + ncol
    f32, i32 = jnp.float32, jnp.int32
    tile = (rows, cols)
    table = conductance.shape[0]
    padded = (npan + 1, rows + SUB, LANES)
    hbm = pl.BlockSpec(memory_space=pltpu.HBM)
    near = pl.BlockSpec(memory_space=pl.ANY)
    outs = pl.pallas_call(
        functools.partial(kernel, nrow, ncol, stages),
        out_shape=(jax.ShapeDtypeStruct(tile, f32), jax.ShapeDtypeStruct(tile, f32)),
        in_specs=[hbm] * 7,
        out_specs=(near, near),
        scratch_shapes=[
            pltpu.VMEM(tile, i32), pltpu.VMEM(tile, i32), pltpu.VMEM(tile, i32),
            pltpu.VMEM(tile, f32), pltpu.VMEM(tile, f32), pltpu.VMEM(tile, f32),
            pltpu.SMEM((table,), f32), pltpu.VMEM((2,) + tile, f32),
            pltpu.VMEM((2,) + padded, f32), pltpu.VMEM((2,) + padded, f32), pltpu.VMEM((2,) + padded, f32),
            pltpu.VMEM(padded, f32), pltpu.VMEM(padded, f32), pltpu.VMEM((npan, rows, LANES), f32),
            pltpu.VMEM((2, 2, npan, SUB, LANES), f32), pltpu.VMEM((2, SUB, LANES), f32),
            pltpu.VMEM((2, 2, npan, SUB, LANES), f32), pltpu.VMEM((6, SUB, LANES), f32),
            pltpu.VMEM((2, 1, LANES), f32), pltpu.VMEM((slots, 1, LANES), f32),
            pltpu.SemaphoreType.DMA((7,)), pltpu.SemaphoreType.DMA((4,)),
            pltpu.SemaphoreType.DMA((8,)), pltpu.SemaphoreType.DMA((8,)),
            pltpu.SemaphoreType.DMA((slots,)), pltpu.SemaphoreType.DMA((slots,)),
        ],
        compiler_params=pltpu.CompilerParams(
            collective_id=0, has_side_effects=True, vmem_limit_bytes=LIMIT),
        name="moments",
    )(wet_mask, land_class, flood_label, conductance, storage, prior_depth, rainfall)
    return pl.pallas_call(
        hand_over,
        out_shape=(jax.ShapeDtypeStruct(tile, f32), jax.ShapeDtypeStruct(tile, f32)),
        in_specs=[near, near],
        out_specs=(near, near),
        scratch_shapes=[pltpu.VMEM((2,) + tile, f32), pltpu.SemaphoreType.DMA((2, 2)), pltpu.SemaphoreType.DMA((2, 2))],
        compiler_params=pltpu.CompilerParams(vmem_limit_bytes=LIMIT),
        name="hand_over",
    )(*outs)


def solution(mesh):
    spread = P(("basin", "row"), "col")
    return jax.shard_map(
        functools.partial(body, mesh.shape["row"], mesh.shape["col"]),
        mesh=mesh,
        in_specs=(spread, spread, spread, P(), spread, spread, spread),
        out_specs=(spread, spread),
        check_vma=False,
    )
```

```python
import functools

import jax
import jax.numpy as jnp
from jax import lax
from jax.experimental import pallas as pl
from jax.experimental.pallas import tpu as pltpu
from jax.sharding import PartitionSpec as P

MESH = pl.DeviceIdType.MESH
LANES = 128
SUB = 8
PIECE = 4
LIMIT = 63500 * 1024
STEPS = (
    (-1, 0), (1, 0), (0, -1), (0, 1), (-1, -1), (-1, 1), (1, -1), (1, 1),
)
OPPOSITE = (1, 0, 3, 2, 7, 6, 5, 4)


def lookup(index, table):
    values = [table[i] for i in range(table.shape[0])]
    bit = 1
    while len(values) > 1:
        odd = (index & bit) != 0
        values = [jnp.where(odd, values[i + 1], values[i]) for i in range(0, len(values), 2)]
        bit *= 2
    return values[0]


def iota(shape, dim):
    return lax.broadcasted_iota(jnp.int32, shape, dim)


def fold(values):
    rows, lanes = values.shape
    return values.reshape(rows // SUB, SUB, lanes).sum(axis=0)


def coefficients(m, c):
    n = [c * m[k] + m[k + 1] for k in range(5)]
    a0 = m[0] / n[0]
    r0, r1 = 1.0 - a0 * c, -a0
    rr1 = r0 * r0 * m[0] + 2.0 * r0 * r1 * m[1] + r1 * r1 * m[2]
    p0, p1 = r0 + rr1 / m[0], r1
    curve = p0 * p0 * n[0] + 2.0 * p0 * p1 * n[1] + p1 * p1 * n[2]
    a1 = rr1 / curve
    u0, u1 = a0 + a1 * p0, a1 * p1
    r0, r1, r2 = r0 - a1 * c * p0, r1 - a1 * (p0 + c * p1), -a1 * p1
    rr2 = (r0 * r0 * m[0] + 2.0 * r0 * r1 * m[1] + (r1 * r1 + 2.0 * r0 * r2) * m[2]
           + 2.0 * r1 * r2 * m[3] + r2 * r2 * m[4])
    beta = rr2 / rr1
    p0, p1, p2 = r0 + beta * p0, r1 + beta * p1, r2
    curve = (p0 * p0 * n[0] + 2.0 * p0 * p1 * n[1] + (p1 * p1 + 2.0 * p0 * p2) * n[2]
             + 2.0 * p1 * p2 * n[3] + p2 * p2 * n[4])
    a2 = rr2 / curve
    return u0 + a2 * p0, u1 + a2 * p1, a2 * p2


def kernel(
    nrow, ncol, stages,
    wet_h, land_h, label_h, cond_h, stor_h, prior_h, rain_h, out0_h, out1_h,
    wet_v, land_v, label_v, stor_v, prior_v, rain_v, cond, out_v,
    v0, v1, v2, cell_s, diag_s, diag_in,
    pack_rows, pack_cols, got_rows, got_cols, part, got_part,
    in_sem, out_sem, send_sem, recv_sem, psend_sem, precv_sem,
):
    rows, cols = stor_v.shape
    nb, npan = rows // SUB, cols // LANES
    row, col = lax.axis_index("row"), lax.axis_index("col")

    loads = [
        pltpu.make_async_copy(src, dst, in_sem.at[i])
        for i, (src, dst) in enumerate((
            (land_h, land_v), (wet_h, wet_v), (stor_h, stor_v),
            (prior_h, prior_v), (rain_h, rain_v), (label_h, label_v), (cond_h, cond)))
    ]
    for load in loads:
        load.start()

    got_rows[...] = jnp.zeros_like(got_rows)
    got_cols[...] = jnp.zeros_like(got_cols)

    there = []
    for dr, dc in STEPS:
        ok = True
        for at, d, n in ((row, dr, nrow), (col, dc, ncol)):
            if d:
                here = (at > 0) if d < 0 else (at < n - 1)
                ok = here if ok is True else jnp.logical_and(ok, here)
        there.append(ok)

    def place(k):
        dr, dc = STEPS[k]
        return {"row": row + dr, "col": col + dc}

    def peer(stage, k):
        if stage == "both":
            at = lax.rem(row * ncol + col + k, nrow * ncol)
            return {"row": at // ncol, "col": lax.rem(at, ncol)}
        if stage == "col":
            return {"row": row, "col": lax.rem(col + k, ncol)}
        return {"row": lax.rem(row + k, nrow), "col": col}

    counts = {"both": nrow * ncol, "row": nrow, "col": ncol}
    barrier = pltpu.get_barrier_semaphore()
    expect = 0
    for stage in stages:
        for k in range(1, counts[stage]):
            pl.semaphore_signal(barrier, inc=1, device_id=peer(stage, k), device_id_type=MESH)
        expect += counts[stage] - 1
    if "both" not in stages:
        for k in range(4, 8):
            @pl.when(there[k])
            def _():
                pl.semaphore_signal(barrier, inc=1, device_id=place(k), device_id_type=MESH)
            expect = expect + there[k].astype(jnp.int32)

    for load in loads:
        load.wait()
    shift = cond[0]
    for i in range(1, cond.shape[0]):
        shift = shift + cond[i]
    shift = shift * (2.0 / cond.shape[0])
    shift = shift * shift


    def prepare(j, low, count):
        at = pl.ds(j * LANES, LANES)
        core = pl.ds(low, count)
        wet = wet_v[core, at].astype(jnp.float32)
        prior = prior_v[core, at]
        stor = stor_v[core, at]
        cell_s[j, core, :] = lookup(land_v[core, at], cond) * wet
        v0[0, j, core, :] = stor * prior + wet * rain_v[core, at]
        v0[1, j, core, :] = wet * (1.0 / (1.0 + jnp.exp(-prior)) - label_v[core, at].astype(jnp.float32))
        diag_s[j, core, :] = stor

    for j in range(npan):
        if 0 < j < npan - 1:
            prepare(j, 0, SUB)
            prepare(j, rows - SUB, SUB)
        else:
            prepare(j, 0, rows)

    fields = (v0.at[0], v0.at[1], cell_s, diag_s)
    sub = iota((SUB, LANES), 0)
    lane = iota((SUB, LANES), 1)
    upper = sub < PIECE
    halves = lane < LANES // 2

    for pair in range(2):
        fa, fb = fields[2 * pair], fields[2 * pair + 1]
        for j in range(npan):
            top = pl.ds(0, SUB)
            bottom = pl.ds(rows - SUB, SUB)
            pack_rows[0, pair, j] = jnp.where(upper, fa[j, top, :], pltpu.roll(fb[j, top, :], PIECE, 0))
            pack_rows[1, pair, j] = jnp.where(upper, pltpu.roll(fa[j, bottom, :], PIECE, 0), fb[j, bottom, :])

    left = jnp.zeros((SUB, LANES), jnp.float32)
    right = jnp.zeros((SUB, LANES), jnp.float32)
    slot = lane // PIECE
    for f, field in enumerate(fields):
        for r in range(nb):
            k = f * nb + r
            block = pl.ds(r * SUB, SUB)
            left = jnp.where(slot == k, pltpu.roll(field[0, block, :], PIECE * k, 1), left)
            right = jnp.where(
                slot == k, pltpu.roll(field[npan - 1, block, :], (PIECE * k + PIECE) % LANES, 1), right)
    pack_cols[0] = left
    pack_cols[1] = right

    pl.semaphore_wait(barrier, expect)

    def halo(k, arriving):
        dr, dc = STEPS[k]
        to = k if arriving else OPPOSITE[k]
        if dc == 0:
            src, dst = pack_rows.at[k], got_rows.at[to]
        else:
            src, dst = pack_cols.at[(dc + 1) // 2], got_cols.at[to - 2]
        return pltpu.make_async_remote_copy(
            src_ref=src, dst_ref=dst, send_sem=send_sem.at[k], recv_sem=recv_sem.at[to],
            device_id=place(k), device_id_type=MESH)

    for k in range(8):
        @pl.when(there[k])
        def _():
            halo(k, False).start()
    for j in range(1, npan - 1):
        prepare(j, SUB, rows - 2 * SUB)

    def around(panels):
        tall, total = panels[0].shape[0], len(panels)
        first = iota((tall, LANES), 1) == 0
        last = iota((tall, LANES), 1) == LANES - 1
        fwd = [pltpu.roll(w, 1, 1) for w in panels]
        bwd = [pltpu.roll(w, LANES - 1, 1) for w in panels]
        return [
            pltpu.roll(w, 1, 0) + pltpu.roll(w, tall - 1, 0)
            + jnp.where(first, fwd[(j - 1) % total], fwd[j])
            + jnp.where(last, bwd[(j + 1) % total], bwd[j])
            for j, w in enumerate(panels)
        ]

    def dots(a, b, total):
        term = fold(a * b)
        return term if total is None else total + term

    def gather(m, step, field, image):
        if step == 0:
            m[0] = dots(field, field, m[0])
        m[2 * step + 1] = dots(field, image, m[2 * step + 1])
        if step < 2:
            m[2 * step + 2] = dots(image, image, m[2 * step + 2])

    whole = pl.ds(0, rows)
    middle = pl.ds(SUB, rows - 2 * SUB)
    inside = slice(SUB, rows - SUB)
    nears = around([cell_s[j, whole, :] for j in range(npan)])
    for j in range(npan):
        diag_in[j] = diag_s[j, whole, :] + cell_s[j, whole, :] * nears[j] - shift
    moments = [[None] * 6, [None] * 6]
    for s in range(2):
        for step, (src, dst) in enumerate(((v0, v1), (v1, v2), (v2, None))):
            nears = around([cell_s[j, whole, :] * src[s, j, whole, :] for j in range(npan)])
            for j in range(npan):
                deep = 0 < j < npan - 1
                if dst is None and not deep:
                    continue
                field = src[s, j, whole, :]
                image = diag_in[j] * field - cell_s[j, whole, :] * nears[j]
                if dst is not None:
                    dst[s, j, whole, :] = image
                if deep:
                    gather(moments[s], step, field[inside], image[inside])

    for k in range(8):
        @pl.when(there[k])
        def _():
            halo(k, True).wait_recv()

    tail = pl.ds(rows, SUB)
    for f, field in enumerate(fields):
        pair, second = f // 2, f % 2
        for j in range(npan):
            after, before = got_rows[1, pair, j], got_rows[0, pair, j]
            if second:
                after = pltpu.roll(after, PIECE, 0)
            else:
                before = pltpu.roll(before, PIECE, 0)
            field[j, tail, :] = jnp.where(upper, after, before)

        def side(after, before, r):
            k = f * nb + r
            after = pltpu.roll(after, (LANES - PIECE * k) % LANES, 1)
            before = pltpu.roll(before, LANES - PIECE - PIECE * k, 1)
            return jnp.where(halves, after, before)

        for r in range(nb):
            field[npan, pl.ds(r * SUB, SUB), :] = side(got_cols[1], got_cols[0], r)
        field[npan, tail, :] = jnp.where(
            upper, side(got_cols[5], got_cols[4], 0), side(got_cols[3], got_cols[2], nb - 1))

    ring = [npan - 2, npan - 1, npan, 0, 1]

    def wide(field, j):
        return jnp.concatenate(
            [field[j, pl.ds(rows - 2 * SUB, 3 * SUB), :], field[j, pl.ds(0, 2 * SUB), :]], axis=0)

    def narrow(field, j):
        return jnp.concatenate(
            [field[j, pl.ds(rows - SUB, 2 * SUB), :], field[j, pl.ds(0, SUB), :]], axis=0)

    def put(field, j, value):
        field[j, pl.ds(rows - SUB, 2 * SUB), :] = value[:2 * SUB]
        field[j, pl.ds(0, SUB), :] = value[2 * SUB:]

    def ends(value):
        return jnp.concatenate([value[:SUB], value[2 * SUB:]], axis=0)

    nears = around([wide(cell_s, j) for j in range(npan + 1)])
    for j in range(npan + 1):
        value = narrow(diag_s, j) + narrow(cell_s, j) * nears[j][SUB:4 * SUB] - shift
        put(diag_s, j, value)
    nears = around([cell_s[j, whole, :] for j in ring])
    for j, near in zip(ring[1:4], nears[1:4]):
        diag_s[j, middle, :] = diag_s[j, middle, :] + cell_s[j, middle, :] * near[SUB:rows - SUB] - shift
    for s in range(2):
        m = moments[s]
        for step, (src, dst) in enumerate(((v0, v1), (v1, v2), (v2, None))):
            nears = around([wide(cell_s, j) * wide(src.at[s], j) for j in range(npan + 1)])
            for j in range(npan + 1):
                if dst is None and j == npan:
                    continue
                field = narrow(src.at[s], j)
                image = narrow(diag_s, j) * field - narrow(cell_s, j) * nears[j][SUB:4 * SUB]
                if dst is not None:
                    put(dst.at[s], j, image)
                if j < npan:
                    gather(m, step, ends(field), ends(image))
            nears = around([cell_s[j, whole, :] * src[s, j, whole, :] for j in ring])
            for j, near in zip(ring[1:4], nears[1:4]):
                if dst is None and j == npan:
                    continue
                field = src[s, j, middle, :]
                image = diag_s[j, middle, :] * field - cell_s[j, middle, :] * near[SUB:rows - SUB]
                if dst is not None:
                    dst[s, j, middle, :] = image
                if j < npan:
                    gather(m, step, field, image)

    gap = jnp.zeros((2, LANES), jnp.float32)
    spread = [jnp.sum(x, axis=0, keepdims=True) for x in moments[0]] + [gap]
    spread += [jnp.sum(x, axis=0, keepdims=True) for x in moments[1]] + [gap]
    spread = jnp.concatenate(spread, axis=0)
    on = iota((2 * SUB, LANES), 0) == iota((2 * SUB, LANES), 1)
    sums = jnp.sum(spread, axis=1, keepdims=True)
    sums = jnp.sum(jnp.where(on, sums, 0.0), axis=0, keepdims=True)

    base = 0
    for number, stage in enumerate(stages):
        part[number] = sums
        copies = []
        for k in range(1, counts[stage]):
            copies.append(pltpu.make_async_remote_copy(
                src_ref=part.at[number], dst_ref=got_part.at[base + k],
                send_sem=psend_sem.at[base + k], recv_sem=precv_sem.at[base + k],
                device_id=peer(stage, k), device_id_type=MESH))
            copies[-1].start()
        for copy in copies:
            copy.wait_recv()
        for k in range(1, counts[stage]):
            sums = sums + got_part[base + k]
        for copy in copies:
            copy.wait_send()
        base += counts[stage]

    sums = jnp.sum(jnp.where(on, sums, 0.0), axis=1, keepdims=True)
    sums = jnp.broadcast_to(sums, (2 * SUB, LANES))
    stores = []
    for s, out_h in enumerate((out0_h, out1_h)):
        m = [sums[s * SUB + i:s * SUB + i + 1] for i in range(6)]
        e0, e1, e2 = coefficients(m, shift)
        for half in range(2):
            low = half * (rows // 2)
            core = pl.ds(low, rows // 2)
            for j in range(npan):
                out_v[s, core, pl.ds(j * LANES, LANES)] = (
                    e0 * v0[s, j, core, :] + e1 * v1[s, j, core, :] + e2 * v2[s, j, core, :])
            stores.append(pltpu.make_async_copy(out_v.at[s, core], out_h.at[core], out_sem.at[2 * s + half]))
            stores[-1].start()
    for k in range(8):
        @pl.when(there[k])
        def _():
            halo(k, False).wait_send()
    for store in stores:
        store.wait()


def hand_over(a_h, b_h, out0_h, out1_h, held, sem, out_sem):
    loads, stores = [], []
    for s, (src, dst) in enumerate(((a_h, out0_h), (b_h, out1_h))):
        for h in range(2):
            at = pl.ds(h * (src.shape[0] // 2), src.shape[0] // 2)
            loads.append(pltpu.make_async_copy(src.at[at], held.at[s, at], sem.at[s, h]))
            stores.append(pltpu.make_async_copy(held.at[s, at], dst.at[at], out_sem.at[s, h]))
            loads[-1].start()
    for load, store in zip(loads, stores):
        load.wait()
        store.start()
    for store in stores:
        store.wait()


def body(nrow, ncol, wet_mask, land_class, flood_label, conductance, storage, prior_depth, rainfall):
    rows, cols = storage.shape
    nb, npan = rows // SUB, cols // LANES
    stages = ("both",) if nrow * ncol <= 32 else ("col", "row")
    slots = nrow * ncol if len(stages) == 1 else nrow + ncol
    f32, i32 = jnp.float32, jnp.int32
    tile = (rows, cols)
    table = conductance.shape[0]
    padded = (npan + 1, rows + SUB, LANES)
    hbm = pl.BlockSpec(memory_space=pltpu.HBM)
    near = pl.BlockSpec(memory_space=pl.ANY)
    outs = pl.pallas_call(
        functools.partial(kernel, nrow, ncol, stages),
        out_shape=(jax.ShapeDtypeStruct(tile, f32), jax.ShapeDtypeStruct(tile, f32)),
        in_specs=[hbm] * 7,
        out_specs=(near, near),
        scratch_shapes=[
            pltpu.VMEM(tile, i32), pltpu.VMEM(tile, i32), pltpu.VMEM(tile, i32),
            pltpu.VMEM(tile, f32), pltpu.VMEM(tile, f32), pltpu.VMEM(tile, f32),
            pltpu.SMEM((table,), f32), pltpu.VMEM((2,) + tile, f32),
            pltpu.VMEM((2,) + padded, f32), pltpu.VMEM((2,) + padded, f32), pltpu.VMEM((2,) + padded, f32),
            pltpu.VMEM(padded, f32), pltpu.VMEM(padded, f32), pltpu.VMEM((npan, rows, LANES), f32),
            pltpu.VMEM((2, 2, npan, SUB, LANES), f32), pltpu.VMEM((2, SUB, LANES), f32),
            pltpu.VMEM((2, 2, npan, SUB, LANES), f32), pltpu.VMEM((6, SUB, LANES), f32),
            pltpu.VMEM((2, 1, LANES), f32), pltpu.VMEM((slots, 1, LANES), f32),
            pltpu.SemaphoreType.DMA((7,)), pltpu.SemaphoreType.DMA((4,)),
            pltpu.SemaphoreType.DMA((8,)), pltpu.SemaphoreType.DMA((8,)),
            pltpu.SemaphoreType.DMA((slots,)), pltpu.SemaphoreType.DMA((slots,)),
        ],
        compiler_params=pltpu.CompilerParams(
            collective_id=0, has_side_effects=True, vmem_limit_bytes=LIMIT),
        name="moments",
    )(wet_mask, land_class, flood_label, conductance, storage, prior_depth, rainfall)
    return pl.pallas_call(
        hand_over,
        out_shape=(jax.ShapeDtypeStruct(tile, f32), jax.ShapeDtypeStruct(tile, f32)),
        in_specs=[near, near],
        out_specs=(near, near),
        scratch_shapes=[pltpu.VMEM((2,) + tile, f32), pltpu.SemaphoreType.DMA((2, 2)), pltpu.SemaphoreType.DMA((2, 2))],
        compiler_params=pltpu.CompilerParams(vmem_limit_bytes=LIMIT),
        name="hand_over",
    )(*outs)


def solution(mesh):
    spread = P(("basin", "row"), "col")
    return jax.shard_map(
        functools.partial(body, mesh.shape["row"], mesh.shape["col"]),
        mesh=mesh,
        in_specs=(spread, spread, spread, P(), spread, spread, spread),
        out_specs=(spread, spread),
        check_vma=False,
    )
```

```python
import functools

import jax
import jax.numpy as jnp
from jax import lax
from jax.experimental import pallas as pl
from jax.experimental.pallas import tpu as pltpu
from jax.sharding import PartitionSpec as P

MESH = pl.DeviceIdType.MESH
LANES = 128
SUB = 8
PIECE = 4
LIMIT = 63500 * 1024
STEPS = (
    (-1, 0), (1, 0), (0, -1), (0, 1), (-1, -1), (-1, 1), (1, -1), (1, 1),
)
OPPOSITE = (1, 0, 3, 2, 7, 6, 5, 4)


def lookup(index, table):
    values = [table[i] for i in range(table.shape[0])]
    bit = 1
    while len(values) > 1:
        odd = (index & bit) != 0
        values = [jnp.where(odd, values[i + 1], values[i]) for i in range(0, len(values), 2)]
        bit *= 2
    return values[0]


def iota(shape, dim):
    return lax.broadcasted_iota(jnp.int32, shape, dim)


def fold(values):
    rows, lanes = values.shape
    return values.reshape(rows // SUB, SUB, lanes).sum(axis=0)


def coefficients(m, c):
    n = [c * m[k] + m[k + 1] for k in range(5)]
    a0 = m[0] / n[0]
    r0, r1 = 1.0 - a0 * c, -a0
    rr1 = r0 * r0 * m[0] + 2.0 * r0 * r1 * m[1] + r1 * r1 * m[2]
    p0, p1 = r0 + rr1 / m[0], r1
    curve = p0 * p0 * n[0] + 2.0 * p0 * p1 * n[1] + p1 * p1 * n[2]
    a1 = rr1 / curve
    u0, u1 = a0 + a1 * p0, a1 * p1
    r0, r1, r2 = r0 - a1 * c * p0, r1 - a1 * (p0 + c * p1), -a1 * p1
    rr2 = (r0 * r0 * m[0] + 2.0 * r0 * r1 * m[1] + (r1 * r1 + 2.0 * r0 * r2) * m[2]
           + 2.0 * r1 * r2 * m[3] + r2 * r2 * m[4])
    beta = rr2 / rr1
    p0, p1, p2 = r0 + beta * p0, r1 + beta * p1, r2
    curve = (p0 * p0 * n[0] + 2.0 * p0 * p1 * n[1] + (p1 * p1 + 2.0 * p0 * p2) * n[2]
             + 2.0 * p1 * p2 * n[3] + p2 * p2 * n[4])
    a2 = rr2 / curve
    return u0 + a2 * p0, u1 + a2 * p1, a2 * p2


def kernel(
    nrow, ncol, stages,
    wet_h, land_h, label_h, cond_h, stor_h, prior_h, rain_h, out0_h, out1_h,
    wet_v, land_v, label_v, stor_v, prior_v, rain_v, cond, out_v,
    v0, v1, v2, cell_s, diag_s, diag_in,
    pack_rows, pack_cols, got_rows, got_cols, part, got_part,
    in_sem, out_sem, send_sem, recv_sem, psend_sem, precv_sem,
):
    rows, cols = stor_v.shape
    nb, npan = rows // SUB, cols // LANES
    row, col = lax.axis_index("row"), lax.axis_index("col")

    loads = [
        pltpu.make_async_copy(src, dst, in_sem.at[i])
        for i, (src, dst) in enumerate((
            (land_h, land_v), (wet_h, wet_v), (stor_h, stor_v),
            (prior_h, prior_v), (rain_h, rain_v), (label_h, label_v), (cond_h, cond)))
    ]
    for load in loads:
        load.start()

    got_rows[...] = jnp.zeros_like(got_rows)
    got_cols[...] = jnp.zeros_like(got_cols)

    there = []
    for dr, dc in STEPS:
        ok = True
        for at, d, n in ((row, dr, nrow), (col, dc, ncol)):
            if d:
                here = (at > 0) if d < 0 else (at < n - 1)
                ok = here if ok is True else jnp.logical_and(ok, here)
        there.append(ok)

    def place(k):
        dr, dc = STEPS[k]
        return {"row": row + dr, "col": col + dc}

    def peer(stage, k):
        if stage == "both":
            at = lax.rem(row * ncol + col + k, nrow * ncol)
            return {"row": at // ncol, "col": lax.rem(at, ncol)}
        if stage == "col":
            return {"row": row, "col": lax.rem(col + k, ncol)}
        return {"row": lax.rem(row + k, nrow), "col": col}

    counts = {"both": nrow * ncol, "row": nrow, "col": ncol}
    barrier = pltpu.get_barrier_semaphore()
    expect = 0
    for stage in stages:
        for k in range(1, counts[stage]):
            pl.semaphore_signal(barrier, inc=1, device_id=peer(stage, k), device_id_type=MESH)
        expect += counts[stage] - 1
    if "both" not in stages:
        for k in range(4, 8):
            @pl.when(there[k])
            def _():
                pl.semaphore_signal(barrier, inc=1, device_id=place(k), device_id_type=MESH)
            expect = expect + there[k].astype(jnp.int32)

    for load in loads:
        load.wait()
    shift = cond[0]
    for i in range(1, cond.shape[0]):
        shift = shift + cond[i]
    shift = shift * (2.0 / cond.shape[0])
    shift = shift * shift

    for j in range(npan):
        at = pl.ds(j * LANES, LANES)
        wet = wet_v[:, at].astype(jnp.float32)
        prior = prior_v[:, at]
        stor = stor_v[:, at]
        core = pl.ds(0, rows)
        cell_s[j, core, :] = lookup(land_v[:, at], cond) * wet
        v0[0, j, core, :] = stor * prior + wet * rain_v[:, at]
        v0[1, j, core, :] = wet * (1.0 / (1.0 + jnp.exp(-prior)) - label_v[:, at].astype(jnp.float32))
        diag_s[j, core, :] = stor

    fields = (v0.at[0], v0.at[1], cell_s, diag_s)
    sub = iota((SUB, LANES), 0)
    lane = iota((SUB, LANES), 1)
    upper = sub < PIECE
    halves = lane < LANES // 2

    for pair in range(2):
        fa, fb = fields[2 * pair], fields[2 * pair + 1]
        for j in range(npan):
            top = pl.ds(0, SUB)
            bottom = pl.ds(rows - SUB, SUB)
            pack_rows[0, pair, j] = jnp.where(upper, fa[j, top, :], pltpu.roll(fb[j, top, :], PIECE, 0))
            pack_rows[1, pair, j] = jnp.where(upper, pltpu.roll(fa[j, bottom, :], PIECE, 0), fb[j, bottom, :])

    left = jnp.zeros((SUB, LANES), jnp.float32)
    right = jnp.zeros((SUB, LANES), jnp.float32)
    slot = lane // PIECE
    for f, field in enumerate(fields):
        for r in range(nb):
            k = f * nb + r
            block = pl.ds(r * SUB, SUB)
            left = jnp.where(slot == k, pltpu.roll(field[0, block, :], PIECE * k, 1), left)
            right = jnp.where(
                slot == k, pltpu.roll(field[npan - 1, block, :], (PIECE * k + PIECE) % LANES, 1), right)
    pack_cols[0] = left
    pack_cols[1] = right

    pl.semaphore_wait(barrier, expect)

    def halo(k, arriving):
        dr, dc = STEPS[k]
        to = k if arriving else OPPOSITE[k]
        if dc == 0:
            src, dst = pack_rows.at[k], got_rows.at[to]
        else:
            src, dst = pack_cols.at[(dc + 1) // 2], got_cols.at[to - 2]
        return pltpu.make_async_remote_copy(
            src_ref=src, dst_ref=dst, send_sem=send_sem.at[k], recv_sem=recv_sem.at[to],
            device_id=place(k), device_id_type=MESH)

    for k in range(8):
        @pl.when(there[k])
        def _():
            halo(k, False).start()
    def around(panels):
        tall, total = panels[0].shape[0], len(panels)
        first = iota((tall, LANES), 1) == 0
        last = iota((tall, LANES), 1) == LANES - 1
        fwd = [pltpu.roll(w, 1, 1) for w in panels]
        bwd = [pltpu.roll(w, LANES - 1, 1) for w in panels]
        return [
            pltpu.roll(w, 1, 0) + pltpu.roll(w, tall - 1, 0)
            + jnp.where(first, fwd[(j - 1) % total], fwd[j])
            + jnp.where(last, bwd[(j + 1) % total], bwd[j])
            for j, w in enumerate(panels)
        ]

    def dots(a, b, total):
        term = fold(a * b)
        return term if total is None else total + term

    def gather(m, step, field, image):
        if step == 0:
            m[0] = dots(field, field, m[0])
        m[2 * step + 1] = dots(field, image, m[2 * step + 1])
        if step < 2:
            m[2 * step + 2] = dots(image, image, m[2 * step + 2])

    whole = pl.ds(0, rows)
    middle = pl.ds(SUB, rows - 2 * SUB)
    inside = slice(SUB, rows - SUB)
    nears = around([cell_s[j, whole, :] for j in range(npan)])
    for j in range(npan):
        diag_in[j] = diag_s[j, whole, :] + cell_s[j, whole, :] * nears[j] - shift
    moments = [[None] * 6, [None] * 6]
    for s in range(2):
        for step, (src, dst) in enumerate(((v0, v1), (v1, v2), (v2, None))):
            nears = around([cell_s[j, whole, :] * src[s, j, whole, :] for j in range(npan)])
            for j in range(npan):
                deep = 0 < j < npan - 1
                if dst is None and not deep:
                    continue
                field = src[s, j, whole, :]
                image = diag_in[j] * field - cell_s[j, whole, :] * nears[j]
                if dst is not None:
                    dst[s, j, whole, :] = image
                if deep:
                    gather(moments[s], step, field[inside], image[inside])

    for k in range(8):
        @pl.when(there[k])
        def _():
            halo(k, True).wait_recv()

    tail = pl.ds(rows, SUB)
    for f, field in enumerate(fields):
        pair, second = f // 2, f % 2
        for j in range(npan):
            after, before = got_rows[1, pair, j], got_rows[0, pair, j]
            if second:
                after = pltpu.roll(after, PIECE, 0)
            else:
                before = pltpu.roll(before, PIECE, 0)
            field[j, tail, :] = jnp.where(upper, after, before)

        def side(after, before, r):
            k = f * nb + r
            after = pltpu.roll(after, (LANES - PIECE * k) % LANES, 1)
            before = pltpu.roll(before, LANES - PIECE - PIECE * k, 1)
            return jnp.where(halves, after, before)

        for r in range(nb):
            field[npan, pl.ds(r * SUB, SUB), :] = side(got_cols[1], got_cols[0], r)
        field[npan, tail, :] = jnp.where(
            upper, side(got_cols[5], got_cols[4], 0), side(got_cols[3], got_cols[2], nb - 1))

    ring = [npan - 2, npan - 1, npan, 0, 1]

    def wide(field, j):
        return jnp.concatenate(
            [field[j, pl.ds(rows - 2 * SUB, 3 * SUB), :], field[j, pl.ds(0, 2 * SUB), :]], axis=0)

    def narrow(field, j):
        return jnp.concatenate(
            [field[j, pl.ds(rows - SUB, 2 * SUB), :], field[j, pl.ds(0, SUB), :]], axis=0)

    def put(field, j, value):
        field[j, pl.ds(rows - SUB, 2 * SUB), :] = value[:2 * SUB]
        field[j, pl.ds(0, SUB), :] = value[2 * SUB:]

    def ends(value):
        return jnp.concatenate([value[:SUB], value[2 * SUB:]], axis=0)

    nears = around([wide(cell_s, j) for j in range(npan + 1)])
    for j in range(npan + 1):
        value = narrow(diag_s, j) + narrow(cell_s, j) * nears[j][SUB:4 * SUB] - shift
        put(diag_s, j, value)
    nears = around([cell_s[j, whole, :] for j in ring])
    for j, near in zip(ring[1:4], nears[1:4]):
        diag_s[j, middle, :] = diag_s[j, middle, :] + cell_s[j, middle, :] * near[SUB:rows - SUB] - shift
    for s in range(2):
        m = moments[s]
        for step, (src, dst) in enumerate(((v0, v1), (v1, v2), (v2, None))):
            nears = around([wide(cell_s, j) * wide(src.at[s], j) for j in range(npan + 1)])
            for j in range(npan + 1):
                if dst is None and j == npan:
                    continue
                field = narrow(src.at[s], j)
                image = narrow(diag_s, j) * field - narrow(cell_s, j) * nears[j][SUB:4 * SUB]
                if dst is not None:
                    put(dst.at[s], j, image)
                if j < npan:
                    gather(m, step, ends(field), ends(image))
            nears = around([cell_s[j, whole, :] * src[s, j, whole, :] for j in ring])
            for j, near in zip(ring[1:4], nears[1:4]):
                if dst is None and j == npan:
                    continue
                field = src[s, j, middle, :]
                image = diag_s[j, middle, :] * field - cell_s[j, middle, :] * near[SUB:rows - SUB]
                if dst is not None:
                    dst[s, j, middle, :] = image
                if j < npan:
                    gather(m, step, field, image)

    gap = jnp.zeros((2, LANES), jnp.float32)
    spread = [jnp.sum(x, axis=0, keepdims=True) for x in moments[0]] + [gap]
    spread += [jnp.sum(x, axis=0, keepdims=True) for x in moments[1]] + [gap]
    spread = jnp.concatenate(spread, axis=0)
    on = iota((2 * SUB, LANES), 0) == iota((2 * SUB, LANES), 1)
    sums = jnp.sum(spread, axis=1, keepdims=True)
    sums = jnp.sum(jnp.where(on, sums, 0.0), axis=0, keepdims=True)

    base = 0
    for number, stage in enumerate(stages):
        part[number] = sums
        copies = []
        for k in range(1, counts[stage]):
            copies.append(pltpu.make_async_remote_copy(
                src_ref=part.at[number], dst_ref=got_part.at[base + k],
                send_sem=psend_sem.at[base + k], recv_sem=precv_sem.at[base + k],
                device_id=peer(stage, k), device_id_type=MESH))
            copies[-1].start()
        for copy in copies:
            copy.wait_recv()
        for k in range(1, counts[stage]):
            sums = sums + got_part[base + k]
        for copy in copies:
            copy.wait_send()
        base += counts[stage]

    sums = jnp.sum(jnp.where(on, sums, 0.0), axis=1, keepdims=True)
    sums = jnp.broadcast_to(sums, (2 * SUB, LANES))
    stores = []
    for s, out_h in enumerate((out0_h, out1_h)):
        m = [sums[s * SUB + i:s * SUB + i + 1] for i in range(6)]
        e0, e1, e2 = coefficients(m, shift)
        for half in range(2):
            low = half * (rows // 2)
            core = pl.ds(low, rows // 2)
            for j in range(npan):
                out_v[s, core, pl.ds(j * LANES, LANES)] = (
                    e0 * v0[s, j, core, :] + e1 * v1[s, j, core, :] + e2 * v2[s, j, core, :])
            stores.append(pltpu.make_async_copy(out_v.at[s, core], out_h.at[core], out_sem.at[2 * s + half]))
            stores[-1].start()
    for k in range(8):
        @pl.when(there[k])
        def _():
            halo(k, False).wait_send()
    for store in stores:
        store.wait()


def hand_over(a_h, b_h, out0_h, out1_h, held, sem, out_sem):
    loads, stores = [], []
    for s, (src, dst) in enumerate(((a_h, out0_h), (b_h, out1_h))):
        for h in range(4):
            at = pl.ds(h * (src.shape[0] // 4), src.shape[0] // 4)
            loads.append(pltpu.make_async_copy(src.at[at], held.at[s, at], sem.at[s, h]))
            stores.append(pltpu.make_async_copy(held.at[s, at], dst.at[at], out_sem.at[s, h]))
            loads[-1].start()
    for load, store in zip(loads, stores):
        load.wait()
        store.start()
    for store in stores:
        store.wait()


def body(nrow, ncol, wet_mask, land_class, flood_label, conductance, storage, prior_depth, rainfall):
    rows, cols = storage.shape
    nb, npan = rows // SUB, cols // LANES
    stages = ("both",) if nrow * ncol <= 32 else ("col", "row")
    slots = nrow * ncol if len(stages) == 1 else nrow + ncol
    f32, i32 = jnp.float32, jnp.int32
    tile = (rows, cols)
    table = conductance.shape[0]
    padded = (npan + 1, rows + SUB, LANES)
    hbm = pl.BlockSpec(memory_space=pltpu.HBM)
    near = pl.BlockSpec(memory_space=pl.ANY)
    outs = pl.pallas_call(
        functools.partial(kernel, nrow, ncol, stages),
        out_shape=(jax.ShapeDtypeStruct(tile, f32), jax.ShapeDtypeStruct(tile, f32)),
        in_specs=[hbm] * 7,
        out_specs=(near, near),
        scratch_shapes=[
            pltpu.VMEM(tile, i32), pltpu.VMEM(tile, i32), pltpu.VMEM(tile, i32),
            pltpu.VMEM(tile, f32), pltpu.VMEM(tile, f32), pltpu.VMEM(tile, f32),
            pltpu.SMEM((table,), f32), pltpu.VMEM((2,) + tile, f32),
            pltpu.VMEM((2,) + padded, f32), pltpu.VMEM((2,) + padded, f32), pltpu.VMEM((2,) + padded, f32),
            pltpu.VMEM(padded, f32), pltpu.VMEM(padded, f32), pltpu.VMEM((npan, rows, LANES), f32),
            pltpu.VMEM((2, 2, npan, SUB, LANES), f32), pltpu.VMEM((2, SUB, LANES), f32),
            pltpu.VMEM((2, 2, npan, SUB, LANES), f32), pltpu.VMEM((6, SUB, LANES), f32),
            pltpu.VMEM((2, 1, LANES), f32), pltpu.VMEM((slots, 1, LANES), f32),
            pltpu.SemaphoreType.DMA((7,)), pltpu.SemaphoreType.DMA((4,)),
            pltpu.SemaphoreType.DMA((8,)), pltpu.SemaphoreType.DMA((8,)),
            pltpu.SemaphoreType.DMA((slots,)), pltpu.SemaphoreType.DMA((slots,)),
        ],
        compiler_params=pltpu.CompilerParams(
            collective_id=0, has_side_effects=True, vmem_limit_bytes=LIMIT),
        name="moments",
    )(wet_mask, land_class, flood_label, conductance, storage, prior_depth, rainfall)
    return pl.pallas_call(
        hand_over,
        out_shape=(jax.ShapeDtypeStruct(tile, f32), jax.ShapeDtypeStruct(tile, f32)),
        in_specs=[near, near],
        out_specs=(near, near),
        scratch_shapes=[pltpu.VMEM((2,) + tile, f32), pltpu.SemaphoreType.DMA((2, 4)), pltpu.SemaphoreType.DMA((2, 4))],
        compiler_params=pltpu.CompilerParams(vmem_limit_bytes=LIMIT),
        name="hand_over",
    )(*outs)


def solution(mesh):
    spread = P(("basin", "row"), "col")
    return jax.shard_map(
        functools.partial(body, mesh.shape["row"], mesh.shape["col"]),
        mesh=mesh,
        in_specs=(spread, spread, spread, P(), spread, spread, spread),
        out_specs=(spread, spread),
        check_vma=False,
    )
```
